256 devices in a mesh: row: 8 (over x, core), col: 32 (over z, y).
Axes of the slice: x: 4, y: 4, z: 8, core: 2. Of those that a mesh axis runs over, the one named last changes fastest.
Arguments:
- adj_trailing: bfloat16 [8192, 32768], P('row', 'col'), may hold values from -6 to 6
- panel_rows0: bfloat16 [8192, 512], P('row'), may hold values from -0.0625 to 0.0625
- panel_rows1: bfloat16 [8192, 512], P('row'), may hold values from -0.0625 to 0.0625
- panel_cols0: bfloat16 [32768, 512], P('col'), may hold values from -0.03125 to 0.03125
- panel_cols1: bfloat16 [32768, 512], P('col'), may hold values from -0.03125 to 0.03125
- inv_diag0: float32 [512, 512], replicated, as said below
- inv_diag1: float32 [512, 512], replicated, as said below
- cross_block: float32 [512, 512], replicated, may hold values from -0.25 to 0.25
- panel_adj0: bfloat16 [8192, 512], P(('row', 'col')), may hold values from -6 to 6
- panel_adj1: bfloat16 [8192, 512], P(('row', 'col')), may hold values from -6 to 6
Outputs:
- row_adj1: float32 [8192, 512], P(('row', 'col'))
- row_adj0: float32 [8192, 512], P(('row', 'col'))
- col_adj1: float32 [32768, 512], P('col')
- col_adj0: float32 [32768, 512], P('col')
- diag_adj1: float32 [512, 512], replicated
- diag_adj0: float32 [512, 512], replicated
The draws below stay inside these ranges and needn't reach their ends.
Inputs may be any that keep to these rules, and one draw needn't show every extreme that they name: `inv_diag0`: lower triangular, with diagonal entries of 1 to 2. `inv_diag1`: lower triangular, with diagonal entries of 1 to 2.
All inputs are finite; a program needn't handle non-finite values.
Results may differ from the reference program's by a relative error of at most 0.0003.
Values sent between devices are 32-bit elements; how exact they have to be, the bound alone decides.
A program may use at most 128 MiB of HBM per device.

```python
import math
import jax
import jax.numpy as jnp
from jax import lax

B = 512
ROWS = 8192
COLS = 32768


def inverse_factor(key):
    first, second = jax.random.split(key)
    index = jnp.arange(B)
    lower = index[:, None] > index[None, :]
    spread = jax.random.normal(first, (B, B), jnp.float32) * (0.6 / math.sqrt(B))
    diagonal = jax.random.uniform(second, (B,), jnp.float32, 1.0, 2.0)
    return jnp.where(lower, spread, 0.0) + jnp.diag(diagonal)


def draw_inv_diag0(key, part):
    return inverse_factor(jax.random.fold_in(key, 11))


def draw_inv_diag1(key, part):
    return inverse_factor(jax.random.fold_in(key, 23))


def levels(rng, dims, pieces, low, top_value):
    def one(axis_at, shards_of):
        draws = jax.random.uniform(jax.random.fold_in(jax.random.fold_in(rng, 6), axis_at), (shards_of,), jnp.float32, low / len(pieces), top_value / len(pieces))
        return jnp.repeat(jnp.exp(draws), dims[axis_at] // shards_of).reshape((-1,) + (1,) * (len(dims) - axis_at - 1))

    factor_of = one(*pieces[0])
    for cut in pieces[1:]:
        factor_of = factor_of * one(*cut)
    return factor_of


def scatter_about(rng, shape, width, bound, pieces=(), kind=jnp.bfloat16):
    factor_of = levels(rng, shape, pieces, -0.22, 0.18) if pieces else 1.0
    array = jax.random.normal(rng, shape, jnp.float32) * width * factor_of
    return jnp.minimum(jnp.maximum(array, -bound), bound).astype(kind)


def setup_inputs(seed: int = 0) -> dict:
    arg_keys = jax.random.split(jax.random.key(seed), 11)
    adj_trailing = scatter_about(arg_keys[0], (ROWS, COLS), 1.0, 6.0, ((0, 8), (1, 32)))
    panel_rows0 = scatter_about(arg_keys[1], (ROWS, B), ROWS ** -0.5, 0.0625, ((0, 8),))
    panel_rows1 = scatter_about(arg_keys[2], (ROWS, B), ROWS ** -0.5, 0.0625, ((0, 8),))
    panel_cols0 = scatter_about(arg_keys[3], (COLS, B), COLS ** -0.5, 0.03125, ((0, 32),))
    panel_cols1 = scatter_about(arg_keys[4], (COLS, B), COLS ** -0.5, 0.03125, ((0, 32),))
    inv_diag0 = draw_inv_diag0(jax.random.fold_in(arg_keys[10], 71), 0)
    inv_diag1 = draw_inv_diag1(jax.random.fold_in(arg_keys[10], 71), 0)
    cross_block = scatter_about(arg_keys[7], (B, B), B ** -0.5, 0.25, (), jnp.float32)
    panel_adj0 = scatter_about(arg_keys[8], (ROWS, B), 1.0, 6.0, ((0, 256),))
    panel_adj1 = scatter_about(arg_keys[9], (ROWS, B), 1.0, 6.0, ((0, 256),))
    return {"adj_trailing": adj_trailing, "panel_rows0": panel_rows0, "panel_rows1": panel_rows1, "panel_cols0": panel_cols0, "panel_cols1": panel_cols1, "inv_diag0": inv_diag0, "inv_diag1": inv_diag1, "cross_block": cross_block, "panel_adj0": panel_adj0, "panel_adj1": panel_adj1}


def reference(adj_trailing, panel_rows0, panel_rows1, panel_cols0, panel_cols1, inv_diag0, inv_diag1, cross_block, panel_adj0, panel_adj1):
    highest = lax.Precision.HIGHEST
    trail1 = jnp.dot(adj_trailing, panel_cols1, preferred_element_type=jnp.float32)
    trail0 = jnp.dot(adj_trailing, panel_cols0, preferred_element_type=jnp.float32)
    col_adj1 = -jnp.einsum("rc,rb->cb", adj_trailing, panel_rows1, preferred_element_type=jnp.float32)
    col_adj0 = -jnp.einsum("rc,rb->cb", adj_trailing, panel_rows0, preferred_element_type=jnp.float32)
    bar1 = panel_adj1.astype(jnp.float32) - trail1
    row_adj1 = jnp.dot(bar1, inv_diag1, precision=highest)
    bar0 = panel_adj0.astype(jnp.float32) - trail0 - jnp.dot(row_adj1, cross_block, precision=highest)
    row_adj0 = jnp.dot(bar0, inv_diag0, precision=highest)
    gram1 = jnp.dot(bar1.T, panel_rows1.astype(jnp.float32), precision=highest)
    gram0 = jnp.dot(bar0.T, panel_rows0.astype(jnp.float32), precision=highest)
    diag_adj1 = -jnp.tril(jnp.dot(inv_diag1.T, gram1, precision=highest))
    diag_adj0 = -jnp.tril(jnp.dot(inv_diag0.T, gram0, precision=highest))
    return (row_adj1, row_adj0, col_adj1, col_adj0, diag_adj1, diag_adj0)
```

```python
import jax
import jax.numpy as jnp
from jax import lax
from jax.experimental import pallas as pl
from jax.experimental.pallas import tpu as pltpu
from jax.sharding import Mesh
from jax.sharding import PartitionSpec as P

AXES = ("x", "core", "z", "y")
SIZES = (4, 2, 8, 4)
ROW = ("x", "core")
COL = ("z", "y")
F32 = jnp.float32
BF16 = jnp.bfloat16
VMEM_LIMIT = 46 << 20
HIGHEST = lax.Precision.HIGHEST
TILES = [(i, j) for i in range(4) for j in range(i + 1)]

Z_FIRST = 1

ORDER = (
    *("a1", "b0", "x3", "x1", "x2", "x0", "g", "a1", "m", "d1", "a0", "d0", "a1", "x1", "d1", "x0",),
    *("d0", "a0", "x3", "x1", "b1", "b0", "d1", "a0", "d0", "d1", "x0", "a0", "x1", "b1", "d1", "d0",),
    *("a1", "x2", "x3", "x0", "b0", "d0", "a1", "b0", "d1", "x1", "x2", "a0", "b1", "a1", "x3", "x1",),
    *("b0", "b1", "d0", "x0", "b0", "b1", "d1", "x2", "a1", "a0", "x3", "d1", "b1", "x2", "b0", "x0",),
    *("d0", "x3", "a0", "b1", "r", "x2", "d0",),
)


def dot(a, b):
    return jnp.dot(a, b, preferred_element_type=F32)


def dot_t(a, b):
    return lax.dot_general(a, b, (((0,), (0,)), ((), ())), preferred_element_type=F32)


def dot_f32(a, b):
    return jnp.dot(a, b, precision=HIGHEST, preferred_element_type=F32)


def split(v):
    high = v.astype(BF16)
    return high, (v - high.astype(F32)).astype(BF16)


def dot_t2(a, b):
    high, low = split(b)
    return dot_t(a, high) + dot_t(a, low)


def dot_t3(a, b):
    ah, al = split(a)
    bh, bl = split(b)
    return dot_t(ah, bh) + (dot_t(ah, bl) + dot_t(al, bh))


def plus(axis, step):
    size = SIZES[AXES.index(axis)]
    return lax.rem(lax.axis_index(axis) + (size + step), size)


def kernel(
    a_in, r0_in, r1_in, k0_in, k1_in, inv0_in, inv1_in, cross_in, p0_in, p1_in,
    col, d_all, rows,
    a_v, r_v, k_v, inv1, inv0, cross, p1_v, p0_v,
    c_send, c_recv, c_sum, x1_recv, x2_recv,
    t_z, zz_recv, t_zy, zy1_recv, zy2_recv,
    t_y, yy1_recv, yy2_recv, t_yz, yz_recv, trail,
    g_v, d_part, d_core, d_sum, d_y, dy_recv, dz_recv, d_x,
    local_sem, send_sem, recv_sem,
):
    x, core, z, y = (lax.axis_index(axis) for axis in AXES)
    xp, xm, xf = plus("x", 1), plus("x", -1), plus("x", 2)
    yp, ym, yf = plus("y", 1), plus("y", -1), plus("y", 2)
    other = 1 - core
    sent, locals_ = [], []

    def send(src, dst, **peer):
        at = len(sent)
        copy = pltpu.make_async_remote_copy(
            src_ref=src, dst_ref=dst, send_sem=send_sem.at[at], recv_sem=recv_sem.at[at],
            device_id=peer, device_id_type=pl.DeviceIdType.MESH,
        )
        copy.start()
        sent.append(copy)
        return copy

    def copy_in(src, dst):
        copy = pltpu.make_async_copy(src, dst, local_sem.at[len(locals_)])
        copy.start()
        locals_.append(copy)
        return copy

    in_r = [copy_in(r1_in, r_v.at[:, 0:512]), copy_in(r0_in, r_v.at[:, 512:1024])]
    in_a = copy_in(a_in, a_v)
    in_k = [copy_in(k1_in, k_v.at[:, 0:512]), copy_in(k0_in, k_v.at[:, 512:1024])]
    in_p = [copy_in(p1_in, p1_v), copy_in(p0_in, p0_v)]
    in_m = [copy_in(inv1_in, inv1), copy_in(cross_in, cross), copy_in(inv0_in, inv0)]

    barrier = pltpu.get_barrier_semaphore()
    peers = [{"core": other}]
    peers += [{"x": plus("x", s)} for s in (1, 2, 3)]
    peers += [{"y": plus("y", s)} for s in (1, 2, 3)]
    peers += [{"z": plus("z", s)} for s in range(1, 8)]
    for peer in peers:
        pl.semaphore_signal(barrier, inc=1, device_id=peer, device_id_type=pl.DeviceIdType.MESH)

    def half(index):
        return pl.ds(pl.multiple_of(index * 512, 512), 512)

    for copy in (*in_r, in_a):
        copy.wait()
    to_core = []
    for j in range(4):
        c_send[j] = -dot_t(a_v[:, half(other)], r_v[:, 256 * j : 256 * j + 256])
        if j == 0:
            pl.semaphore_wait(barrier, len(peers))
        to_core.append(send(c_send.at[j], c_recv.at[j], core=other))
    for j in range(4):
        c_sum[j] = -dot_t(a_v[:, half(core)], r_v[:, 256 * j : 256 * j + 256])

    def rows_at(index, size, extra=0, count=None):
        start = pl.multiple_of(index * size + extra, 8)
        return pl.ds(start, size if count is None else count)

    def x_stream(j):
        to_core[j].wait_recv()
        c_sum[j] = c_sum[j] + c_recv[j]
        p = send(c_sum.at[j, rows_at(xf, 128, 0, 64)], x1_recv.at[j, 0], x=xp)
        m = send(c_sum.at[j, rows_at(xf, 128, 64, 64)], x1_recv.at[j, 1], x=xm)
        yield
        p.wait_recv()
        at = rows_at(xp, 128, 0, 64)
        c_sum[j, at] = c_sum[j, at] + x1_recv[j, 0]
        p = send(c_sum.at[j, rows_at(xp, 128)], x2_recv.at[j, 0], x=xp)
        m.wait_recv()
        at = rows_at(xm, 128, 64, 64)
        c_sum[j, at] = c_sum[j, at] + x1_recv[j, 1]
        m = send(c_sum.at[j, rows_at(xm, 128)], x2_recv.at[j, 1], x=xm)
        yield
        p.wait_recv()
        m.wait_recv()
        base = core * 512
        own = pl.ds(pl.multiple_of(base + x * 128, 128), 128)
        col[j, own] = c_sum[j, rows_at(x, 128)] + x2_recv[j, 0] + x2_recv[j, 1]
        p = send(col.at[j, own], col.at[j, own], x=xp)
        m = send(col.at[j, own], col.at[j, own], x=xm)
        yield
        p.wait_recv()
        at = pl.ds(pl.multiple_of(base + xm * 128, 64), 64)
        p = send(col.at[j, at], col.at[j, at], x=xp)
        m.wait_recv()
        at = pl.ds(pl.multiple_of(base + xp * 128 + 64, 64), 64)
        m = send(col.at[j, at], col.at[j, at], x=xm)
        yield
        p.wait_recv()
        m.wait_recv()
        c = send(col.at[j, half(core)], col.at[j, half(core)], core=other)
        yield
        c.wait_recv()
        yield

    def z_ring(q, recv, size):
        h = size // 2
        far = plus("z", 4)
        p = send(q.at[far, 0:h], recv.at[0, 0, 0:h], z=plus("z", 1))
        m = send(q.at[far, h:size], recv.at[1, 0, 0:h], z=plus("z", -1))
        yield
        for s in (1, 2, 3):
            to_p, to_m = plus("z", 4 - s), plus("z", s - 4)
            p.wait_recv()
            if s == 1:
                q[to_p, 0:h] = q[to_p, 0:h] + recv[0, 0, 0:h]
            else:
                q[to_p] = q[to_p] + recv[0, s - 1]
            p = send(q.at[to_p], recv.at[0, s], z=plus("z", 1))
            m.wait_recv()
            if s == 1:
                q[to_m, h:size] = q[to_m, h:size] + recv[1, 0, 0:h]
            else:
                q[to_m] = q[to_m] + recv[1, s - 1]
            m = send(q.at[to_m], recv.at[1, s], z=plus("z", -1))
            yield
        p.wait_recv()
        m.wait_recv()

    z_panel, y_panel = (0, 1) if Z_FIRST == 1 else (1, 0)

    def a_stream(i):
        lanes = slice(256 * i, 256 * i + 256)
        first = 512 * z_panel + 256 * i
        t, ty = t_z.at[i], t_zy.at[i]
        t[...] = dot(a_v[...], k_v[:, first : first + 256]).reshape(8, 128, 256)
        yield from z_ring(t, zz_recv.at[i], 128)
        ty[...] = (t[z] + zz_recv[i, 0, 3] + zz_recv[i, 1, 3]).reshape(4, 32, 256)
        p = send(ty.at[yf, 0:16], zy1_recv.at[i, 0], y=yp)
        m = send(ty.at[yf, 16:32], zy1_recv.at[i, 1], y=ym)
        yield
        p.wait_recv()
        ty[yp, 0:16] = ty[yp, 0:16] + zy1_recv[i, 0]
        p = send(ty.at[yp], zy2_recv.at[i, 0], y=yp)
        m.wait_recv()
        ty[ym, 16:32] = ty[ym, 16:32] + zy1_recv[i, 1]
        m = send(ty.at[ym], zy2_recv.at[i, 1], y=ym)
        yield
        p.wait_recv()
        m.wait_recv()
        trail[z_panel, :, lanes] = ty[y] + zy2_recv[i, 0] + zy2_recv[i, 1]
        yield

    def b_stream(i):
        lanes = slice(256 * i, 256 * i + 256)
        first = 512 * y_panel + 256 * i
        t, tz = t_y.at[i], t_yz.at[i]
        t[...] = dot(a_v[...], k_v[:, first : first + 256]).reshape(8, 4, 32, 256)
        p = send(t.at[0:4, yf], yy1_recv.at[i, 0], y=yp)
        m = send(t.at[4:8, yf], yy1_recv.at[i, 1], y=ym)
        yield
        p.wait_recv()
        t[0:4, yp] = t[0:4, yp] + yy1_recv[i, 0]
        p = send(t.at[:, yp], yy2_recv.at[i, 0], y=yp)
        m.wait_recv()
        t[4:8, ym] = t[4:8, ym] + yy1_recv[i, 1]
        m = send(t.at[:, ym], yy2_recv.at[i, 1], y=ym)
        yield
        p.wait_recv()
        m.wait_recv()
        tz[...] = t[:, y] + yy2_recv[i, 0] + yy2_recv[i, 1]
        yield from z_ring(tz, yz_recv.at[i], 32)
        trail[y_panel, :, lanes] = tz[z] + yz_recv[i, 0, 3] + yz_recv[i, 1, 3]
        yield

    def gram():
        at = pl.ds(pl.multiple_of((z * 4 + y) * 32, 32), 32)
        k1, k0 = k_v[half(core), 0:512], k_v[half(core), 512:1024]
        r1, r0 = r_v[at, 0:512], r_v[at, 512:1024]
        p1, p0 = p1_v[...], p0_v[...]
        g_v[0, :, 0:256] = dot_t2(k1, c_sum[0]) + dot_t(p1, r1[:, 0:256])
        g_v[0, 256:512, 256:512] = dot_t2(k1[:, 256:512], c_sum[1]) + dot_t(p1[:, 256:512], r1[:, 256:512])
        for j in (0, 1):
            lanes = slice(256 * j, 256 * j + 256)
            g_v[1, :, lanes] = dot_t2(k1, c_sum[2 + j]) + dot_t(p1, r0[:, lanes])
        g_v[2, :, 0:256] = dot_t2(k0, c_sum[2]) + dot_t(p0, r0[:, 0:256])
        g_v[2, 256:512, 256:512] = dot_t2(k0[:, 256:512], c_sum[3]) + dot_t(p0[:, 256:512], r0[:, 256:512])

    def lower_t(inv, g, whole):
        upper = dot_t3(inv[:, 0:256], g[:, 0:512] if whole else g[:, 0:256])
        lower = dot_t3(inv[256:512, 256:512], g[256:512, 0:512])
        return upper, lower

    def put_tiles(at, upper, lower):
        for index, (i, j) in enumerate(TILES):
            v = upper if i < 2 else lower
            v = v[128 * (i % 2) : 128 * (i % 2) + 128, 128 * j : 128 * j + 128]
            if i == j:
                row = lax.broadcasted_iota(jnp.int32, (128, 128), 0)
                lane = lax.broadcasted_iota(jnp.int32, (128, 128), 1)
                v = jnp.where(row >= lane, v, 0.0)
            d_part[at, 128 * index : 128 * index + 128] = -v

    def local_diag():
        put_tiles(0, *lower_t(inv1[...], g_v[0], False))
        w_upper, w_lower = lower_t(inv1[...], g_v[1], True)
        g_v[1, 0:256] = w_upper
        g_v[1, 256:512] = w_lower
        g_v[2, :, 0:256] = g_v[2, :, 0:256] - dot_t3(cross[...], g_v[1, :, 0:256])
        g_v[2, 256:512, 256:512] = g_v[2, 256:512, 256:512] - dot_t3(cross[:, 256:512], g_v[1, :, 256:512])
        put_tiles(1, *lower_t(inv0[...], g_v[2], False))

    def d_stream(i):
        size, base = (768, 512)[i], (0, 768)[i]
        ny, nz = size // 4, size // 32
        whole, by, bz = pl.ds(base, size), pl.ds(base // 4, ny), pl.ds(base // 32, nz)

        def of_y(index, start):
            return pl.ds(pl.multiple_of(start + index * ny, 8), ny)

        def of_z(index, start):
            return pl.ds(pl.multiple_of(start + index * nz, 8), nz)

        c = send(d_part.at[other, whole], d_core.at[whole], core=other)
        yield
        c.wait_recv()
        d_sum[whole] = d_part[core, whole] + d_core[whole]
        cs = [send(d_sum.at[of_y(plus("y", s), base)], dy_recv.at[s - 1, by], y=plus("y", s)) for s in (1, 2, 3)]
        yield
        for c in cs:
            c.wait_recv()
        d_y[by] = d_sum[of_y(y, base)] + dy_recv[0, by] + dy_recv[1, by] + dy_recv[2, by]
        cs = [send(d_y.at[of_z(plus("z", s), base // 4)], dz_recv.at[s - 1, bz], z=plus("z", s)) for s in range(1, 8)]
        yield
        for c in cs:
            c.wait_recv()
        total = d_y[of_z(z, base // 4)]
        for s in range(7):
            total = total + dz_recv[s, bz]
        d_x[x, bz] = total
        cs = [send(d_x.at[x, bz], d_x.at[x, bz], x=plus("x", s)) for s in (1, 2, 3)]
        yield
        for c in cs:
            c.wait_recv()
        own = pl.ds(pl.multiple_of(base + y * ny + z * nz, 8), nz)
        d_all[core, own] = (d_x[0, bz] + d_x[1, bz]) + (d_x[2, bz] + d_x[3, bz])
        cs = [send(d_all.at[core, own], d_all.at[core, own], z=plus("z", s)) for s in range(1, 8)]
        yield
        for c in cs:
            c.wait_recv()
        own = of_y(y, base)
        cs = [send(d_all.at[core, own], d_all.at[core, own], y=plus("y", s)) for s in (1, 2, 3)]
        yield
        for c in cs:
            c.wait_recv()
        c = send(d_all.at[core, whole], d_all.at[core, whole], core=other)
        yield
        c.wait_recv()
        yield

    def row_adjoints():
        bar1 = p1_v[...].astype(F32) - trail[0]
        row1 = dot_f32(bar1, inv1[...])
        rows[0] = row1
        bar0 = p0_v[...].astype(F32) - trail[1] - dot_f32(row1, cross[...])
        rows[1] = dot_f32(bar0, inv0[...])

    streams = {"x%d" % j: x_stream(j) for j in range(4)}
    for i in range(2):
        streams.update({"a%d" % i: a_stream(i), "b%d" % i: b_stream(i), "d%d" % i: d_stream(i)})
    loaded = len(in_r) + 1
    for name in ORDER:
        if name[0] in "ab" and loaded < len(locals_):
            for copy in locals_[loaded:]:
                copy.wait()
            loaded = len(locals_)
        if name == "g":
            gram()
        elif name == "m":
            local_diag()
        elif name == "r":
            row_adjoints()
        else:
            next(streams[name])
    for copy in sent:
        copy.wait_send()


def place(col, d_all, rows, row1_out, row0_out, col1_out, col0_out, diag1_out, diag0_out, diag, sem):
    copies = []

    def put(src, dst):
        copy = pltpu.make_async_copy(src, dst, sem.at[len(copies)])
        copy.start()
        copies.append(copy)

    for j in range(4):
        out = (col1_out, col0_out)[j // 2]
        put(col.at[j], out.at[:, 256 * (j % 2) : 256 * (j % 2) + 256])
    put(rows.at[0], row1_out)
    put(rows.at[1], row0_out)
    for panel, out in enumerate((diag1_out, diag0_out)):
        for i in range(3):
            diag[panel, 128 * i : 128 * i + 128, 128 * i + 128 : 512] = jnp.zeros((128, 384 - 128 * i), F32)
        for index, (i, j) in enumerate(TILES):
            tile = d_all[panel, 128 * index : 128 * index + 128]
            diag[panel, 128 * i : 128 * i + 128, 128 * j : 128 * j + 128] = tile
        put(diag.at[panel], out)
    for copy in copies:
        copy.wait()


def local(adj_trailing, panel_rows0, panel_rows1, panel_cols0, panel_cols1, inv_diag0, inv_diag1, cross_block, panel_adj0, panel_adj1):
    anywhere = pl.BlockSpec(memory_space=pltpu.HBM)
    vmem = pl.BlockSpec(memory_space=pltpu.VMEM)
    out = lambda *dims: jax.ShapeDtypeStruct(dims, F32)
    f = lambda *dims: pltpu.VMEM(dims, F32)
    b = lambda *dims: pltpu.VMEM(dims, BF16)
    results = pl.pallas_call(
        kernel,
        out_shape=(f(4, 1024, 256), f(2, 1280, 128), f(2, 32, 512)),
        in_specs=[anywhere] * 10,
        out_specs=(vmem,) * 3,
        scratch_shapes=[
            b(1024, 1024), b(1024, 1024), b(1024, 1024), f(512, 512), f(512, 512), f(512, 512), b(32, 512), b(32, 512),
            f(4, 512, 256), f(4, 512, 256), f(4, 512, 256), f(4, 2, 64, 256), f(4, 2, 128, 256),
            f(2, 8, 128, 256), f(2, 2, 4, 128, 256), f(2, 4, 32, 256), f(2, 2, 16, 256), f(2, 2, 32, 256),
            f(2, 8, 4, 32, 256), f(2, 2, 4, 32, 256), f(2, 2, 8, 32, 256), f(2, 8, 32, 256), f(2, 2, 4, 32, 256), f(2, 32, 512),
            f(3, 512, 512), f(2, 1280, 128), f(1280, 128), f(1280, 128), f(320, 128), f(3, 320, 128),
            f(7, 40, 128), f(4, 40, 128),
            pltpu.SemaphoreType.DMA((16,)), pltpu.SemaphoreType.DMA((152,)), pltpu.SemaphoreType.DMA((152,)),
        ],
        compiler_params=pltpu.CompilerParams(collective_id=0, has_side_effects=True, vmem_limit_bytes=VMEM_LIMIT),
        name="panels",
    )(
        adj_trailing, panel_rows0, panel_rows1, panel_cols0, panel_cols1,
        inv_diag0, inv_diag1, cross_block, panel_adj0, panel_adj1,
    )
    return pl.pallas_call(
        place,
        out_shape=(out(32, 512), out(32, 512), out(1024, 512), out(1024, 512), out(512, 512), out(512, 512)),
        in_specs=[vmem] * 3,
        out_specs=(anywhere,) * 6,
        scratch_shapes=[f(2, 512, 512), pltpu.SemaphoreType.DMA((8,))],
        compiler_params=pltpu.CompilerParams(vmem_limit_bytes=4 << 20),
        name="place",
    )(*results)


def solution(mesh):
    finer = Mesh(mesh.devices.reshape(SIZES), AXES)
    every = (*ROW, *COL)
    in_specs = (
        P(ROW, COL), P(ROW, None), P(ROW, None), P(COL, None), P(COL, None),
        P(), P(), P(), P(every, None), P(every, None),
    )
    out_specs = (P(every, None), P(every, None), P(COL, None), P(COL, None), P(), P())
    return jax.shard_map(local, mesh=finer, in_specs=in_specs, out_specs=out_specs, check_vma=False)
```

```python
import jax
import jax.numpy as jnp
from jax import lax
from jax.experimental import pallas as pl
from jax.experimental.pallas import tpu as pltpu
from jax.sharding import Mesh
from jax.sharding import PartitionSpec as P

AXES = ("x", "core", "z", "y")
SIZES = (4, 2, 8, 4)
ROW = ("x", "core")
COL = ("z", "y")
F32 = jnp.float32
BF16 = jnp.bfloat16
VMEM_LIMIT = 50 << 20
HIGHEST = lax.Precision.HIGHEST
TILES = [(i, j) for i in range(4) for j in range(i + 1)]

Z_FIRST = 1

ORDER = (
    *("a0", "a1", "x0", "x1", "b1", "x2", "x3", "g", "x4", "x5", "b0", "x6", "x7", "h", "a0", "m",),
    *("d1", "x1", "a1", "d0", "x0", "x4", "x2", "d2", "x6", "d1", "a0", "d0", "d2", "x3", "b1", "x1",),
    *("a1", "d1", "x6", "x4", "x5", "b0", "d0", "d2", "a0", "x6", "x1", "a1", "d1", "x2", "x4", "x1",),
    *("d0", "x7", "d1", "b1", "d2", "x2", "a0", "x6", "x0", "x3", "d0", "b0", "a1", "x5", "x4", "x7",),
    *("a0", "b1", "d2", "x0", "d1", "b0", "x1", "x3", "b1", "d0", "x5", "x2", "x6", "b0", "d2", "x0",),
    *("x7", "a1", "x3", "x5", "a0", "d1", "b1", "b0", "x7", "x0", "x5", "d0", "x3", "x4", "d1", "b1",),
    *("d2", "x2", "x7", "a1", "b0", "r", "d0", "d2",),
)


def dot(a, b):
    return jnp.dot(a, b, preferred_element_type=F32)


def dot_t(a, b):
    return lax.dot_general(a, b, (((0,), (0,)), ((), ())), preferred_element_type=F32)


def dot_f32(a, b):
    return jnp.dot(a, b, precision=HIGHEST, preferred_element_type=F32)


def split(v):
    high = v.astype(BF16)
    return high, (v - high.astype(F32)).astype(BF16)


def dot_t2(a, b):
    high, low = split(b)
    return dot_t(a, high) + dot_t(a, low)


def dot_t3(a, b):
    ah, al = split(a)
    bh, bl = split(b)
    return dot_t(ah, bh) + (dot_t(ah, bl) + dot_t(al, bh))


def plus(axis, step):
    size = SIZES[AXES.index(axis)]
    return lax.rem(lax.axis_index(axis) + (size + step), size)


def kernel(
    a_in, r0_in, r1_in, k0_in, k1_in, inv0_in, inv1_in, cross_in, p0_in, p1_in,
    col, d_all, rows,
    a_v, r_v, k_v, inv1, inv0, cross, p1_v, p0_v,
    c_send, c_recv, c_sum, x1_recv, x2_send, x2_recv,
    t_z, zz_recv, t_zy, zy1_recv, zy2_recv,
    t_y, yy1_recv, yy2_recv, t_yz, yz_recv, trail,
    g_v, d_part, d_core, d_sum, d_y, dy_recv, dz_recv, d_x,
    local_sem, send_sem, recv_sem,
):
    x, core, z, y = (lax.axis_index(axis) for axis in AXES)
    xp, xm, xf = plus("x", 1), plus("x", -1), plus("x", 2)
    yp, ym, yf = plus("y", 1), plus("y", -1), plus("y", 2)
    other = 1 - core
    sent, locals_ = [], []

    def send(src, dst, **peer):
        at = len(sent)
        copy = pltpu.make_async_remote_copy(
            src_ref=src, dst_ref=dst, send_sem=send_sem.at[at], recv_sem=recv_sem.at[at],
            device_id=peer, device_id_type=pl.DeviceIdType.MESH,
        )
        copy.start()
        sent.append(copy)
        return copy

    def copy_in(src, dst):
        copy = pltpu.make_async_copy(src, dst, local_sem.at[len(locals_)])
        copy.start()
        locals_.append(copy)
        return copy

    in_r1 = copy_in(r1_in, r_v.at[:, 0:512])
    in_a = copy_in(a_in, a_v)
    in_r0 = copy_in(r0_in, r_v.at[:, 512:1024])

    barrier = pltpu.get_barrier_semaphore()
    peers = [{"core": other}]
    peers += [{"x": plus("x", s)} for s in (1, 2, 3)]
    peers += [{"y": plus("y", s)} for s in (1, 2, 3)]
    peers += [{"z": plus("z", s)} for s in range(1, 8)]
    for peer in peers:
        pl.semaphore_signal(barrier, inc=1, device_id=peer, device_id_type=pl.DeviceIdType.MESH)

    def half(index):
        return pl.ds(pl.multiple_of(index * 512, 512), 512)

    def column_terms(index, j):
        return -dot_t(a_v[:, half(index)], r_v[:, 256 * j : 256 * j + 256])

    in_r1.wait()
    in_a.wait()
    copy_in(k1_in, k_v.at[:, 0:512])
    copy_in(k0_in, k_v.at[:, 512:1024])
    for src, dst in ((p1_in, p1_v), (p0_in, p0_v), (inv1_in, inv1), (cross_in, cross), (inv0_in, inv0)):
        copy_in(src, dst)
    to_core = []
    for j in range(4):
        if j == 2:
            in_r0.wait()
        terms = column_terms(other, j)
        for h in range(2):
            c_send[2 * j + h] = terms[:, 128 * h : 128 * h + 128]
        if j == 0:
            pl.semaphore_wait(barrier, len(peers))
        to_core += [send(c_send.at[at], c_recv.at[at], core=other) for at in (2 * j, 2 * j + 1)]

    def rows_at(index, size, extra=0, count=None):
        start = pl.multiple_of(index * size + extra, 8)
        return pl.ds(start, size if count is None else count)

    def x_stream(j):
        if j % 2 == 0:
            terms = column_terms(core, j // 2)
            c_sum[j] = terms[:, 0:128]
            c_sum[j + 1] = terms[:, 128:256]
        to_core[j].wait_recv()
        c_sum[j] = c_sum[j] + c_recv[j]
        p = send(c_sum.at[j, rows_at(xf, 128, 0, 64)], x1_recv.at[j, 0], x=xp)
        m = send(c_sum.at[j, rows_at(xf, 128, 64, 64)], x1_recv.at[j, 1], x=xm)
        yield
        p.wait_recv()
        x2_send[j, 0, 0:64] = c_sum[j, rows_at(xp, 128, 0, 64)] + x1_recv[j, 0]
        x2_send[j, 0, 64:128] = c_sum[j, rows_at(xp, 128, 64, 64)]
        p = send(x2_send.at[j, 0], x2_recv.at[j, 0], x=xp)
        m.wait_recv()
        x2_send[j, 1, 0:64] = c_sum[j, rows_at(xm, 128, 0, 64)]
        x2_send[j, 1, 64:128] = c_sum[j, rows_at(xm, 128, 64, 64)] + x1_recv[j, 1]
        m = send(x2_send.at[j, 1], x2_recv.at[j, 1], x=xm)
        yield
        p.wait_recv()
        m.wait_recv()
        base = core * 512
        own = pl.ds(pl.multiple_of(base + x * 128, 128), 128)
        col[j, own] = c_sum[j, rows_at(x, 128)] + x2_recv[j, 0] + x2_recv[j, 1]
        p = send(col.at[j, own], col.at[j, own], x=xp)
        m = send(col.at[j, own], col.at[j, own], x=xm)
        yield
        p.wait_recv()
        at = pl.ds(pl.multiple_of(base + xm * 128, 64), 64)
        p = send(col.at[j, at], col.at[j, at], x=xp)
        m.wait_recv()
        at = pl.ds(pl.multiple_of(base + xp * 128 + 64, 64), 64)
        m = send(col.at[j, at], col.at[j, at], x=xm)
        yield
        p.wait_recv()
        m.wait_recv()
        c = send(col.at[j, half(core)], col.at[j, half(core)], core=other)
        yield
        c.wait_recv()
        yield

    def z_ring(q, recv, size):
        h = size // 2
        far = plus("z", 4)
        p = send(q.at[far, 0:h], recv.at[0, 0, 0:h], z=plus("z", 1))
        m = send(q.at[far, h:size], recv.at[1, 0, 0:h], z=plus("z", -1))
        yield
        for s in (1, 2, 3):
            to_p, to_m = plus("z", 4 - s), plus("z", s - 4)
            p.wait_recv()
            if s == 1:
                q[to_p, 0:h] = q[to_p, 0:h] + recv[0, 0, 0:h]
            else:
                q[to_p] = q[to_p] + recv[0, s - 1]
            p = send(q.at[to_p], recv.at[0, s], z=plus("z", 1))
            m.wait_recv()
            if s == 1:
                q[to_m, h:size] = q[to_m, h:size] + recv[1, 0, 0:h]
            else:
                q[to_m] = q[to_m] + recv[1, s - 1]
            m = send(q.at[to_m], recv.at[1, s], z=plus("z", -1))
            yield
        p.wait_recv()
        m.wait_recv()

    z_panel, y_panel = (0, 1) if Z_FIRST == 1 else (1, 0)

    def a_stream(i):
        lanes = slice(256 * i, 256 * i + 256)
        first = 512 * z_panel + 256 * i
        t, ty = t_z.at[i], t_zy.at[i]
        t[...] = dot(a_v[...], k_v[:, first : first + 256]).reshape(8, 128, 256)
        yield from z_ring(t, zz_recv.at[i], 128)
        ty[...] = (t[z] + zz_recv[i, 0, 3] + zz_recv[i, 1, 3]).reshape(4, 32, 256)
        p = send(ty.at[yf, 0:16], zy1_recv.at[i, 0], y=yp)
        m = send(ty.at[yf, 16:32], zy1_recv.at[i, 1], y=ym)
        yield
        p.wait_recv()
        ty[yp, 0:16] = ty[yp, 0:16] + zy1_recv[i, 0]
        p = send(ty.at[yp], zy2_recv.at[i, 0], y=yp)
        m.wait_recv()
        ty[ym, 16:32] = ty[ym, 16:32] + zy1_recv[i, 1]
        m = send(ty.at[ym], zy2_recv.at[i, 1], y=ym)
        yield
        p.wait_recv()
        m.wait_recv()
        trail[z_panel, :, lanes] = ty[y] + zy2_recv[i, 0] + zy2_recv[i, 1]
        yield

    def b_stream(i):
        lanes = slice(256 * i, 256 * i + 256)
        first = 512 * y_panel + 256 * i
        t, tz = t_y.at[i], t_yz.at[i]
        t[...] = dot(a_v[...], k_v[:, first : first + 256]).reshape(8, 4, 32, 256)
        p = send(t.at[0:4, yf], yy1_recv.at[i, 0], y=yp)
        m = send(t.at[4:8, yf], yy1_recv.at[i, 1], y=ym)
        yield
        p.wait_recv()
        t[0:4, yp] = t[0:4, yp] + yy1_recv[i, 0]
        p = send(t.at[:, yp], yy2_recv.at[i, 0], y=yp)
        m.wait_recv()
        t[4:8, ym] = t[4:8, ym] + yy1_recv[i, 1]
        m = send(t.at[:, ym], yy2_recv.at[i, 1], y=ym)
        yield
        p.wait_recv()
        m.wait_recv()
        tz[...] = t[:, y] + yy2_recv[i, 0] + yy2_recv[i, 1]
        yield from z_ring(tz, yz_recv.at[i], 32)
        trail[y_panel, :, lanes] = tz[z] + yz_recv[i, 0, 3] + yz_recv[i, 1, 3]
        yield

    def own_rows():
        return pl.ds(pl.multiple_of((z * 4 + y) * 32, 32), 32)

    def sums(j):
        return jnp.concatenate((c_sum[2 * j], c_sum[2 * j + 1]), axis=1)

    def gram1():
        k1, r1, p1 = k_v[half(core), 0:512], r_v[own_rows(), 0:512], p1_v[...]
        g_v[0, :, 0:256] = dot_t2(k1, sums(0)) + dot_t(p1, r1[:, 0:256])
        g_v[0, 256:512, 256:512] = dot_t2(k1[:, 256:512], sums(1)) + dot_t(p1[:, 256:512], r1[:, 256:512])

    def gram0():
        k1, k0 = k_v[half(core), 0:512], k_v[half(core), 512:1024]
        r0, p1, p0 = r_v[own_rows(), 512:1024], p1_v[...], p0_v[...]
        left, right = sums(2), sums(3)
        g_v[1, :, 0:256] = dot_t2(k1, left) + dot_t(p1, r0[:, 0:256])
        g_v[1, :, 256:512] = dot_t2(k1, right) + dot_t(p1, r0[:, 256:512])
        g_v[2, :, 0:256] = dot_t2(k0, left) + dot_t(p0, r0[:, 0:256])
        g_v[2, 256:512, 256:512] = dot_t2(k0[:, 256:512], right) + dot_t(p0[:, 256:512], r0[:, 256:512])

    def lower_t(inv, g, whole):
        upper = dot_t3(inv[:, 0:256], g[:, 0:512] if whole else g[:, 0:256])
        lower = dot_t3(inv[256:512, 256:512], g[256:512, 0:512])
        return upper, lower

    def put_tiles(at, upper, lower):
        for index, (i, j) in enumerate(TILES):
            v = upper if i < 2 else lower
            v = v[128 * (i % 2) : 128 * (i % 2) + 128, 128 * j : 128 * j + 128]
            if i == j:
                row = lax.broadcasted_iota(jnp.int32, (128, 128), 0)
                lane = lax.broadcasted_iota(jnp.int32, (128, 128), 1)
                v = jnp.where(row >= lane, v, 0.0)
            d_part[at, 128 * index : 128 * index + 128] = -v

    def local_diag():
        put_tiles(0, *lower_t(inv1[...], g_v[0], False))
        w_upper, w_lower = lower_t(inv1[...], g_v[1], True)
        g_v[1, 0:256] = w_upper
        g_v[1, 256:512] = w_lower
        g_v[2, :, 0:256] = g_v[2, :, 0:256] - dot_t3(cross[...], g_v[1, :, 0:256])
        g_v[2, 256:512, 256:512] = g_v[2, 256:512, 256:512] - dot_t3(cross[:, 256:512], g_v[1, :, 256:512])
        put_tiles(1, *lower_t(inv0[...], g_v[2], False))

    def d_stream(i):
        size, base = (512, 512, 256)[i], 512 * i
        ny, nz = size // 4, size // 32
        whole, by, bz = pl.ds(base, size), pl.ds(base // 4, ny), pl.ds(base // 32, nz)

        def of_y(index, start):
            return pl.ds(pl.multiple_of(start + index * ny, 8), ny)

        def of_z(index, start):
            return pl.ds(pl.multiple_of(start + index * nz, 8), nz)

        c = send(d_part.at[other, whole], d_core.at[whole], core=other)
        yield
        c.wait_recv()
        d_sum[whole] = d_part[core, whole] + d_core[whole]
        cs = [send(d_sum.at[of_y(plus("y", s), base)], dy_recv.at[s - 1, by], y=plus("y", s)) for s in (1, 2, 3)]
        yield
        for c in cs:
            c.wait_recv()
        d_y[by] = d_sum[of_y(y, base)] + dy_recv[0, by] + dy_recv[1, by] + dy_recv[2, by]
        cs = [send(d_y.at[of_z(plus("z", s), base // 4)], dz_recv.at[s - 1, bz], z=plus("z", s)) for s in range(1, 8)]
        yield
        for c in cs:
            c.wait_recv()
        total = d_y[of_z(z, base // 4)]
        for s in range(7):
            total = total + dz_recv[s, bz]
        d_x[x, bz] = total
        cs = [send(d_x.at[x, bz], d_x.at[x, bz], x=plus("x", s)) for s in (1, 2, 3)]
        yield
        for c in cs:
            c.wait_recv()
        own = pl.ds(pl.multiple_of(base + y * ny + z * nz, 8), nz)
        d_all[core, own] = (d_x[0, bz] + d_x[1, bz]) + (d_x[2, bz] + d_x[3, bz])
        cs = [send(d_all.at[core, own], d_all.at[core, own], z=plus("z", s)) for s in range(1, 8)]
        yield
        for c in cs:
            c.wait_recv()
        own = of_y(y, base)
        cs = [send(d_all.at[core, own], d_all.at[core, own], y=plus("y", s)) for s in (1, 2, 3)]
        yield
        for c in cs:
            c.wait_recv()
        c = send(d_all.at[core, whole], d_all.at[core, whole], core=other)
        yield
        c.wait_recv()
        yield

    def row_adjoints():
        bar1 = p1_v[...].astype(F32) - trail[0]
        row1 = dot_f32(bar1, inv1[...])
        rows[0] = row1
        bar0 = p0_v[...].astype(F32) - trail[1] - dot_f32(row1, cross[...])
        rows[1] = dot_f32(bar0, inv0[...])

    streams = {"x%d" % j: x_stream(j) for j in range(8)}
    streams.update({"d%d" % i: d_stream(i) for i in range(3)})
    for i in range(2):
        streams.update({"a%d" % i: a_stream(i), "b%d" % i: b_stream(i)})
    loaded = 3
    for name in ORDER:
        if name[0] in "abgh" and loaded < len(locals_):
            for copy in locals_[loaded:]:
                copy.wait()
            loaded = len(locals_)
        if name == "g":
            gram1()
        elif name == "h":
            gram0()
        elif name == "m":
            local_diag()
        elif name == "r":
            row_adjoints()
        else:
            next(streams[name])
    for copy in sent:
        copy.wait_send()


def place(col, d_all, rows, row1_out, row0_out, col1_out, col0_out, diag1_out, diag0_out, diag, sem):
    copies = []

    def put(src, dst):
        copy = pltpu.make_async_copy(src, dst, sem.at[len(copies)])
        copy.start()
        copies.append(copy)

    for j in range(8):
        out = (col1_out, col0_out)[j // 4]
        put(col.at[j], out.at[:, 128 * (j % 4) : 128 * (j % 4) + 128])
    put(rows.at[0], row1_out)
    put(rows.at[1], row0_out)
    for panel, out in enumerate((diag1_out, diag0_out)):
        for i in range(3):
            diag[panel, 128 * i : 128 * i + 128, 128 * i + 128 : 512] = jnp.zeros((128, 384 - 128 * i), F32)
        for index, (i, j) in enumerate(TILES):
            tile = d_all[panel, 128 * index : 128 * index + 128]
            diag[panel, 128 * i : 128 * i + 128, 128 * j : 128 * j + 128] = tile
        put(diag.at[panel], out)
    for copy in copies:
        copy.wait()


def local(adj_trailing, panel_rows0, panel_rows1, panel_cols0, panel_cols1, inv_diag0, inv_diag1, cross_block, panel_adj0, panel_adj1):
    anywhere = pl.BlockSpec(memory_space=pltpu.HBM)
    vmem = pl.BlockSpec(memory_space=pltpu.VMEM)
    out = lambda *dims: jax.ShapeDtypeStruct(dims, F32)
    f = lambda *dims: pltpu.VMEM(dims, F32)
    b = lambda *dims: pltpu.VMEM(dims, BF16)
    results = pl.pallas_call(
        kernel,
        out_shape=(f(8, 1024, 128), f(2, 1280, 128), f(2, 32, 512)),
        in_specs=[anywhere] * 10,
        out_specs=(vmem,) * 3,
        scratch_shapes=[
            b(1024, 1024), b(1024, 1024), b(1024, 1024), f(512, 512), f(512, 512), f(512, 512), b(32, 512), b(32, 512),
            f(8, 512, 128), f(8, 512, 128), f(8, 512, 128), f(8, 2, 64, 128), f(8, 2, 128, 128), f(8, 2, 128, 128),
            f(2, 8, 128, 256), f(2, 2, 4, 128, 256), f(2, 4, 32, 256), f(2, 2, 16, 256), f(2, 2, 32, 256),
            f(2, 8, 4, 32, 256), f(2, 2, 4, 32, 256), f(2, 2, 8, 32, 256), f(2, 8, 32, 256), f(2, 2, 4, 32, 256), f(2, 32, 512),
            f(3, 512, 512), f(2, 1280, 128), f(1280, 128), f(1280, 128), f(320, 128), f(3, 320, 128),
            f(7, 40, 128), f(4, 40, 128),
            pltpu.SemaphoreType.DMA((16,)), pltpu.SemaphoreType.DMA((208,)), pltpu.SemaphoreType.DMA((208,)),
        ],
        compiler_params=pltpu.CompilerParams(collective_id=0, has_side_effects=True, vmem_limit_bytes=VMEM_LIMIT),
        name="panels",
    )(
        adj_trailing, panel_rows0, panel_rows1, panel_cols0, panel_cols1,
        inv_diag0, inv_diag1, cross_block, panel_adj0, panel_adj1,
    )
    return pl.pallas_call(
        place,
        out_shape=(out(32, 512), out(32, 512), out(1024, 512), out(1024, 512), out(512, 512), out(512, 512)),
        in_specs=[vmem] * 3,
        out_specs=(anywhere,) * 6,
        scratch_shapes=[f(2, 512, 512), pltpu.SemaphoreType.DMA((12,))],
        compiler_params=pltpu.CompilerParams(vmem_limit_bytes=4 << 20),
        name="place",
    )(*results)


def solution(mesh):
    finer = Mesh(mesh.devices.reshape(SIZES), AXES)
    every = (*ROW, *COL)
    in_specs = (
        P(ROW, COL), P(ROW, None), P(ROW, None), P(COL, None), P(COL, None),
        P(), P(), P(), P(every, None), P(every, None),
    )
    out_specs = (P(every, None), P(every, None), P(COL, None), P(COL, None), P(), P())
    return jax.shard_map(local, mesh=finer, in_specs=in_specs, out_specs=out_specs, check_vma=False)
```

```python
import jax
import jax.numpy as jnp
from jax import lax
from jax.experimental import pallas as pl
from jax.experimental.pallas import tpu as pltpu
from jax.sharding import Mesh
from jax.sharding import PartitionSpec as P

AXES = ("x", "core", "z", "y")
SIZES = (4, 2, 8, 4)
ROW = ("x", "core")
COL = ("z", "y")
F32 = jnp.float32
BF16 = jnp.bfloat16
VMEM_LIMIT = 50 << 20
HIGHEST = lax.Precision.HIGHEST
TILES = [(i, j) for i in range(4) for j in range(i + 1)]

Z_FIRST = 1

ORDER = (
    *("a1", "b0", "x3", "x1", "x2", "x0", "g", "a1", "m", "d1", "a0", "d0", "a1", "x1", "d1", "x0",),
    *("d0", "a0", "x3", "x1", "b1", "b0", "d1", "a0", "d0", "d1", "x0", "a0", "x1", "b1", "d1", "d0",),
    *("a1", "x2", "x3", "x0", "b0", "d0", "a1", "b0", "d1", "x1", "x2", "a0", "b1", "a1", "x3", "x1",),
    *("b0", "b1", "d0", "x0", "b0", "b1", "d1", "x2", "a1", "a0", "x3", "d1", "b1", "x2", "b0", "x0",),
    *("d0", "x3", "a0", "b1", "r", "x2", "d0",),
)


def dot(a, b):
    return jnp.dot(a, b, preferred_element_type=F32)


def dot_t(a, b):
    return lax.dot_general(a, b, (((0,), (0,)), ((), ())), preferred_element_type=F32)


def dot_f32(a, b):
    return jnp.dot(a, b, precision=HIGHEST, preferred_element_type=F32)


def split(v):
    high = v.astype(BF16)
    return high, (v - high.astype(F32)).astype(BF16)


def dot_t2(a, b):
    high, low = split(b)
    return dot_t(a, high) + dot_t(a, low)


def dot_t3(a, b):
    ah, al = split(a)
    bh, bl = split(b)
    return dot_t(ah, bh) + (dot_t(ah, bl) + dot_t(al, bh))


def plus(axis, step):
    size = SIZES[AXES.index(axis)]
    return lax.rem(lax.axis_index(axis) + (size + step), size)


def kernel(
    a_in, r0_in, r1_in, k0_in, k1_in, inv0_in, inv1_in, cross_in, p0_in, p1_in,
    col, d_all, rows,
    a_v, r_v, k_v, inv1, inv0, cross, p1_v, p0_v,
    c_send, c_recv, c_sum, x1_recv, x2_recv,
    t_z, zz_recv, t_zy, zy1_recv, zy2_recv,
    t_y, yy1_recv, yy2_recv, t_yz, yz_recv, trail,
    g_v, d_part, d_core, d_sum, d_y, dy_recv, dz_recv, d_x,
    local_sem, send_sem, recv_sem,
):
    x, core, z, y = (lax.axis_index(axis) for axis in AXES)
    xp, xm, xf = plus("x", 1), plus("x", -1), plus("x", 2)
    yp, ym, yf = plus("y", 1), plus("y", -1), plus("y", 2)
    other = 1 - core
    sent, locals_ = [], []

    def send(src, dst, **peer):
        at = len(sent)
        copy = pltpu.make_async_remote_copy(
            src_ref=src, dst_ref=dst, send_sem=send_sem.at[at], recv_sem=recv_sem.at[at],
            device_id=peer, device_id_type=pl.DeviceIdType.MESH,
        )
        copy.start()
        sent.append(copy)
        return copy

    def copy_in(src, dst):
        copy = pltpu.make_async_copy(src, dst, local_sem.at[len(locals_)])
        copy.start()
        locals_.append(copy)
        return copy

    in_r = [copy_in(r1_in, r_v.at[:, 0:512]), copy_in(r0_in, r_v.at[:, 512:1024])]
    in_a = copy_in(a_in, a_v)
    in_k = [copy_in(k1_in, k_v.at[:, 0:512]), copy_in(k0_in, k_v.at[:, 512:1024])]
    in_p = [copy_in(p1_in, p1_v), copy_in(p0_in, p0_v)]
    in_m = [copy_in(inv1_in, inv1), copy_in(cross_in, cross), copy_in(inv0_in, inv0)]

    barrier = pltpu.get_barrier_semaphore()
    peers = [{"core": other}]
    peers += [{"x": plus("x", s)} for s in (1, 2, 3)]
    peers += [{"y": plus("y", s)} for s in (1, 2, 3)]
    peers += [{"z": plus("z", s)} for s in range(1, 8)]
    for peer in peers:
        pl.semaphore_signal(barrier, inc=1, device_id=peer, device_id_type=pl.DeviceIdType.MESH)

    def half(index):
        return pl.ds(pl.multiple_of(index * 512, 512), 512)

    for copy in (*in_r, in_a):
        copy.wait()
    to_core = []
    for j in range(4):
        c_send[j] = -dot_t(a_v[:, half(other)], r_v[:, 256 * j : 256 * j + 256])
        if j == 0:
            pl.semaphore_wait(barrier, len(peers))
        to_core.append(send(c_send.at[j], c_recv.at[j], core=other))
    for j in range(4):
        c_sum[j] = -dot_t(a_v[:, half(core)], r_v[:, 256 * j : 256 * j + 256])

    def rows_at(index, size, extra=0, count=None):
        start = pl.multiple_of(index * size + extra, 8)
        return pl.ds(start, size if count is None else count)

    def x_stream(j):
        to_core[j].wait_recv()
        c_sum[j] = c_sum[j] + c_recv[j]
        p = send(c_sum.at[j, rows_at(xf, 128, 0, 64)], x1_recv.at[j, 0], x=xp)
        m = send(c_sum.at[j, rows_at(xf, 128, 64, 64)], x1_recv.at[j, 1], x=xm)
        yield
        p.wait_recv()
        at = rows_at(xp, 128, 0, 64)
        c_sum[j, at] = c_sum[j, at] + x1_recv[j, 0]
        p = send(c_sum.at[j, rows_at(xp, 128)], x2_recv.at[j, 0], x=xp)
        m.wait_recv()
        at = rows_at(xm, 128, 64, 64)
        c_sum[j, at] = c_sum[j, at] + x1_recv[j, 1]
        m = send(c_sum.at[j, rows_at(xm, 128)], x2_recv.at[j, 1], x=xm)
        yield
        p.wait_recv()
        m.wait_recv()
        base = core * 512
        own = pl.ds(pl.multiple_of(base + x * 128, 128), 128)
        col[j, own] = c_sum[j, rows_at(x, 128)] + x2_recv[j, 0] + x2_recv[j, 1]
        p = send(col.at[j, own], col.at[j, own], x=xp)
        m = send(col.at[j, own], col.at[j, own], x=xm)
        yield
        p.wait_recv()
        at = pl.ds(pl.multiple_of(base + xm * 128, 64), 64)
        p = send(col.at[j, at], col.at[j, at], x=xp)
        m.wait_recv()
        at = pl.ds(pl.multiple_of(base + xp * 128 + 64, 64), 64)
        m = send(col.at[j, at], col.at[j, at], x=xm)
        yield
        p.wait_recv()
        m.wait_recv()
        c = send(col.at[j, half(core)], col.at[j, half(core)], core=other)
        yield
        c.wait_recv()
        yield

    def z_ring(q, recv, size):
        h = size // 2
        far = plus("z", 4)
        p = send(q.at[far, 0:h], recv.at[0, 0, 0:h], z=plus("z", 1))
        m = send(q.at[far, h:size], recv.at[1, 0, 0:h], z=plus("z", -1))
        yield
        for s in (1, 2, 3):
            to_p, to_m = plus("z", 4 - s), plus("z", s - 4)
            p.wait_recv()
            if s == 1:
                q[to_p, 0:h] = q[to_p, 0:h] + recv[0, 0, 0:h]
            else:
                q[to_p] = q[to_p] + recv[0, s - 1]
            p = send(q.at[to_p], recv.at[0, s], z=plus("z", 1))
            m.wait_recv()
            if s == 1:
                q[to_m, h:size] = q[to_m, h:size] + recv[1, 0, 0:h]
            else:
                q[to_m] = q[to_m] + recv[1, s - 1]
            m = send(q.at[to_m], recv.at[1, s], z=plus("z", -1))
            yield
        p.wait_recv()
        m.wait_recv()

    z_panel, y_panel = (0, 1) if Z_FIRST == 1 else (1, 0)

    def a_stream(i):
        lanes = slice(256 * i, 256 * i + 256)
        first = 512 * z_panel + 256 * i
        t, ty = t_z.at[i], t_zy.at[i]
        t[...] = dot(a_v[...], k_v[:, first : first + 256]).reshape(8, 128, 256)
        yield from z_ring(t, zz_recv.at[i], 128)
        ty[...] = (t[z] + zz_recv[i, 0, 3] + zz_recv[i, 1, 3]).reshape(4, 32, 256)
        p = send(ty.at[yf, 0:16], zy1_recv.at[i, 0], y=yp)
        m = send(ty.at[yf, 16:32], zy1_recv.at[i, 1], y=ym)
        yield
        p.wait_recv()
        ty[yp, 0:16] = ty[yp, 0:16] + zy1_recv[i, 0]
        p = send(ty.at[yp], zy2_recv.at[i, 0], y=yp)
        m.wait_recv()
        ty[ym, 16:32] = ty[ym, 16:32] + zy1_recv[i, 1]
        m = send(ty.at[ym], zy2_recv.at[i, 1], y=ym)
        yield
        p.wait_recv()
        m.wait_recv()
        trail[z_panel, :, lanes] = ty[y] + zy2_recv[i, 0] + zy2_recv[i, 1]
        yield

    def b_stream(i):
        lanes = slice(256 * i, 256 * i + 256)
        first = 512 * y_panel + 256 * i
        t, tz = t_y.at[i], t_yz.at[i]
        t[...] = dot(a_v[...], k_v[:, first : first + 256]).reshape(8, 4, 32, 256)
        p = send(t.at[0:4, yf], yy1_recv.at[i, 0], y=yp)
        m = send(t.at[4:8, yf], yy1_recv.at[i, 1], y=ym)
        yield
        p.wait_recv()
        t[0:4, yp] = t[0:4, yp] + yy1_recv[i, 0]
        p = send(t.at[:, yp], yy2_recv.at[i, 0], y=yp)
        m.wait_recv()
        t[4:8, ym] = t[4:8, ym] + yy1_recv[i, 1]
        m = send(t.at[:, ym], yy2_recv.at[i, 1], y=ym)
        yield
        p.wait_recv()
        m.wait_recv()
        tz[...] = t[:, y] + yy2_recv[i, 0] + yy2_recv[i, 1]
        yield from z_ring(tz, yz_recv.at[i], 32)
        trail[y_panel, :, lanes] = tz[z] + yz_recv[i, 0, 3] + yz_recv[i, 1, 3]
        yield

    def gram():
        at = pl.ds(pl.multiple_of((z * 4 + y) * 32, 32), 32)
        k1, k0 = k_v[half(core), 0:512], k_v[half(core), 512:1024]
        r1, r0 = r_v[at, 0:512], r_v[at, 512:1024]
        p1, p0 = p1_v[...], p0_v[...]
        g_v[0, :, 0:256] = dot_t2(k1, c_sum[0]) + dot_t(p1, r1[:, 0:256])
        g_v[0, 256:512, 256:512] = dot_t2(k1[:, 256:512], c_sum[1]) + dot_t(p1[:, 256:512], r1[:, 256:512])
        for j in (0, 1):
            lanes = slice(256 * j, 256 * j + 256)
            g_v[1, :, lanes] = dot_t2(k1, c_sum[2 + j]) + dot_t(p1, r0[:, lanes])
        g_v[2, :, 0:256] = dot_t2(k0, c_sum[2]) + dot_t(p0, r0[:, 0:256])
        g_v[2, 256:512, 256:512] = dot_t2(k0[:, 256:512], c_sum[3]) + dot_t(p0[:, 256:512], r0[:, 256:512])

    def lower_t(inv, g, whole):
        upper = dot_t3(inv[:, 0:256], g[:, 0:512] if whole else g[:, 0:256])
        lower = dot_t3(inv[256:512, 256:512], g[256:512, 0:512])
        return upper, lower

    def put_tiles(at, upper, lower):
        for index, (i, j) in enumerate(TILES):
            v = upper if i < 2 else lower
            v = v[128 * (i % 2) : 128 * (i % 2) + 128, 128 * j : 128 * j + 128]
            if i == j:
                row = lax.broadcasted_iota(jnp.int32, (128, 128), 0)
                lane = lax.broadcasted_iota(jnp.int32, (128, 128), 1)
                v = jnp.where(row >= lane, v, 0.0)
            d_part[at, 128 * index : 128 * index + 128] = -v

    def local_diag():
        put_tiles(0, *lower_t(inv1[...], g_v[0], False))
        w_upper, w_lower = lower_t(inv1[...], g_v[1], True)
        g_v[1, 0:256] = w_upper
        g_v[1, 256:512] = w_lower
        g_v[2, :, 0:256] = g_v[2, :, 0:256] - dot_t3(cross[...], g_v[1, :, 0:256])
        g_v[2, 256:512, 256:512] = g_v[2, 256:512, 256:512] - dot_t3(cross[:, 256:512], g_v[1, :, 256:512])
        put_tiles(1, *lower_t(inv0[...], g_v[2], False))

    def d_stream(i):
        size, base = (768, 512)[i], (0, 768)[i]
        ny, nz = size // 4, size // 32
        whole, by, bz = pl.ds(base, size), pl.ds(base // 4, ny), pl.ds(base // 32, nz)

        def of_y(index, start):
            return pl.ds(pl.multiple_of(start + index * ny, 8), ny)

        def of_z(index, start):
            return pl.ds(pl.multiple_of(start + index * nz, 8), nz)

        c = send(d_part.at[other, whole], d_core.at[whole], core=other)
        yield
        c.wait_recv()
        d_sum[whole] = d_part[core, whole] + d_core[whole]
        cs = [send(d_sum.at[of_y(plus("y", s), base)], dy_recv.at[s - 1, by], y=plus("y", s)) for s in (1, 2, 3)]
        yield
        for c in cs:
            c.wait_recv()
        d_y[by] = d_sum[of_y(y, base)] + dy_recv[0, by] + dy_recv[1, by] + dy_recv[2, by]
        cs = [send(d_y.at[of_z(plus("z", s), base // 4)], dz_recv.at[s - 1, bz], z=plus("z", s)) for s in range(1, 8)]
        yield
        for c in cs:
            c.wait_recv()
        total = d_y[of_z(z, base // 4)]
        for s in range(7):
            total = total + dz_recv[s, bz]
        d_x[x, bz] = total
        cs = [send(d_x.at[x, bz], d_x.at[x, bz], x=plus("x", s)) for s in (1, 2, 3)]
        yield
        for c in cs:
            c.wait_recv()
        own = pl.ds(pl.multiple_of(base + y * ny + z * nz, 8), nz)
        d_all[core, own] = (d_x[0, bz] + d_x[1, bz]) + (d_x[2, bz] + d_x[3, bz])
        cs = [send(d_all.at[core, own], d_all.at[core, own], z=plus("z", s)) for s in range(1, 8)]
        yield
        for c in cs:
            c.wait_recv()
        own = of_y(y, base)
        cs = [send(d_all.at[core, own], d_all.at[core, own], y=plus("y", s)) for s in (1, 2, 3)]
        yield
        for c in cs:
            c.wait_recv()
        c = send(d_all.at[core, whole], d_all.at[core, whole], core=other)
        yield
        c.wait_recv()
        yield

    def row_adjoints():
        bar1 = p1_v[...].astype(F32) - trail[0]
        row1 = dot_f32(bar1, inv1[...])
        rows[0] = row1
        bar0 = p0_v[...].astype(F32) - trail[1] - dot_f32(row1, cross[...])
        rows[1] = dot_f32(bar0, inv0[...])

    streams = {"x%d" % j: x_stream(j) for j in range(4)}
    for i in range(2):
        streams.update({"a%d" % i: a_stream(i), "b%d" % i: b_stream(i), "d%d" % i: d_stream(i)})
    loaded = len(in_r) + 1
    for name in ORDER:
        if name[0] in "ab" and loaded < len(locals_):
            for copy in locals_[loaded:]:
                copy.wait()
            loaded = len(locals_)
        if name == "g":
            gram()
        elif name == "m":
            local_diag()
        elif name == "r":
            row_adjoints()
        else:
            next(streams[name])
    for copy in sent:
        copy.wait_send()


def place(col, d_all, rows, row1_out, row0_out, col1_out, col0_out, diag1_out, diag0_out, diag, sem):
    copies = []

    def put(src, dst):
        copy = pltpu.make_async_copy(src, dst, sem.at[len(copies)])
        copy.start()
        copies.append(copy)

    for j in range(4):
        out = (col1_out, col0_out)[j // 2]
        put(col.at[j], out.at[:, 256 * (j % 2) : 256 * (j % 2) + 256])
    put(rows.at[0], row1_out)
    put(rows.at[1], row0_out)
    for panel, out in enumerate((diag1_out, diag0_out)):
        for i in range(3):
            diag[panel, 128 * i : 128 * i + 128, 128 * i + 128 : 512] = jnp.zeros((128, 384 - 128 * i), F32)
        for index, (i, j) in enumerate(TILES):
            tile = d_all[panel, 128 * index : 128 * index + 128]
            diag[panel, 128 * i : 128 * i + 128, 128 * j : 128 * j + 128] = tile
        put(diag.at[panel], out)
    for copy in copies:
        copy.wait()


def local(adj_trailing, panel_rows0, panel_rows1, panel_cols0, panel_cols1, inv_diag0, inv_diag1, cross_block, panel_adj0, panel_adj1):
    anywhere = pl.BlockSpec(memory_space=pltpu.HBM)
    vmem = pl.BlockSpec(memory_space=pltpu.VMEM)
    out = lambda *dims: jax.ShapeDtypeStruct(dims, F32)
    f = lambda *dims: pltpu.VMEM(dims, F32)
    b = lambda *dims: pltpu.VMEM(dims, BF16)
    results = pl.pallas_call(
        kernel,
        out_shape=(f(4, 1024, 256), f(2, 1280, 128), f(2, 32, 512)),
        in_specs=[anywhere] * 10,
        out_specs=(vmem,) * 3,
        scratch_shapes=[
            b(1024, 1024), b(1024, 1024), b(1024, 1024), f(512, 512), f(512, 512), f(512, 512), b(32, 512), b(32, 512),
            f(4, 512, 256), f(4, 512, 256), f(4, 512, 256), f(4, 2, 64, 256), f(4, 2, 128, 256),
            f(2, 8, 128, 256), f(2, 2, 4, 128, 256), f(2, 4, 32, 256), f(2, 2, 16, 256), f(2, 2, 32, 256),
            f(2, 8, 4, 32, 256), f(2, 2, 4, 32, 256), f(2, 2, 8, 32, 256), f(2, 8, 32, 256), f(2, 2, 4, 32, 256), f(2, 32, 512),
            f(3, 512, 512), f(2, 1280, 128), f(1280, 128), f(1280, 128), f(320, 128), f(3, 320, 128),
            f(7, 40, 128), f(4, 40, 128),
            pltpu.SemaphoreType.DMA((16,)), pltpu.SemaphoreType.DMA((152,)), pltpu.SemaphoreType.DMA((152,)),
        ],
        compiler_params=pltpu.CompilerParams(collective_id=0, has_side_effects=True, vmem_limit_bytes=VMEM_LIMIT),
        name="panels",
    )(
        adj_trailing, panel_rows0, panel_rows1, panel_cols0, panel_cols1,
        inv_diag0, inv_diag1, cross_block, panel_adj0, panel_adj1,
    )
    return pl.pallas_call(
        place,
        out_shape=(out(32, 512), out(32, 512), out(1024, 512), out(1024, 512), out(512, 512), out(512, 512)),
        in_specs=[vmem] * 3,
        out_specs=(anywhere,) * 6,
        scratch_shapes=[f(2, 512, 512), pltpu.SemaphoreType.DMA((8,))],
        compiler_params=pltpu.CompilerParams(vmem_limit_bytes=4 << 20),
        name="place",
    )(*results)


def solution(mesh):
    finer = Mesh(mesh.devices.reshape(SIZES), AXES)
    every = (*ROW, *COL)
    in_specs = (
        P(ROW, COL), P(ROW, None), P(ROW, None), P(COL, None), P(COL, None),
        P(), P(), P(), P(every, None), P(every, None),
    )
    out_specs = (P(every, None), P(every, None), P(COL, None), P(COL, None), P(), P())
    return jax.shard_map(local, mesh=finer, in_specs=in_specs, out_specs=out_specs, check_vma=False)
```

```python
import jax
import jax.numpy as jnp
from jax import lax
from jax.experimental import pallas as pl
from jax.experimental.pallas import tpu as pltpu
from jax.sharding import Mesh
from jax.sharding import PartitionSpec as P

AXES = ("x", "core", "z", "y")
SIZES = (4, 2, 8, 4)
ROW = ("x", "core")
COL = ("z", "y")
F32 = jnp.float32
BF16 = jnp.bfloat16
VMEM_LIMIT = 50 << 20
HIGHEST = lax.Precision.HIGHEST
TILES = [(i, j) for i in range(4) for j in range(i + 1)]

Z_FIRST = 1

ORDER = (
    *("b0", "a1", "b1", "x0", "a0", "x1", "x2", "x3", "g", "m", "d1", "a1", "x0", "d0", "d1", "a0",),
    *("x2", "x3", "d0", "a1", "b1", "b0", "a0", "d1", "x2", "x1", "x0", "d0", "a1", "d1", "a0", "x2",),
    *("d0", "x3", "d1", "b1", "a1", "x1", "b0", "d0", "x0", "a0", "a1", "x2", "b1", "b0", "x3", "a0",),
    *("a1", "d1", "x1", "b0", "b1", "x2", "a0", "d0", "x0", "x3", "x1", "b0", "x0", "d1", "b1", "b0",),
    *("d0", "x3", "d1", "b1", "x1", "r", "d0",),
)


def dot(a, b):
    return jnp.dot(a, b, preferred_element_type=F32)


def dot_t(a, b):
    return lax.dot_general(a, b, (((0,), (0,)), ((), ())), preferred_element_type=F32)


def dot_f32(a, b):
    return jnp.dot(a, b, precision=HIGHEST, preferred_element_type=F32)


def split(v):
    high = v.astype(BF16)
    return high, (v - high.astype(F32)).astype(BF16)


def dot_t2(a, b):
    high, low = split(b)
    return dot_t(a, high) + dot_t(a, low)


def dot_t3(a, b):
    ah, al = split(a)
    bh, bl = split(b)
    return dot_t(ah, bh) + (dot_t(ah, bl) + dot_t(al, bh))


def plus(axis, step):
    size = SIZES[AXES.index(axis)]
    return lax.rem(lax.axis_index(axis) + (size + step), size)


def kernel(
    a_in, r0_in, r1_in, k0_in, k1_in, inv0_in, inv1_in, cross_in, p0_in, p1_in,
    col, d_all, rows,
    a_v, r_v, k_v, inv1, inv0, cross, p1_v, p0_v,
    c_send, c_recv, c_sum, x1_recv, x2_recv,
    t_z, zz_recv, t_zy, zy1_recv, zy2_recv,
    t_y, yy1_recv, yy2_recv, t_yz, yz_recv, trail,
    g_v, d_part, d_core, d_sum, d_y, dy_recv, dz_recv, d_x,
    local_sem, send_sem, recv_sem,
):
    x, core, z, y = (lax.axis_index(axis) for axis in AXES)
    xp, xm, xf = plus("x", 1), plus("x", -1), plus("x", 2)
    yp, ym, yf = plus("y", 1), plus("y", -1), plus("y", 2)
    other = 1 - core
    sent, locals_ = [], []

    def send(src, dst, **peer):
        at = len(sent)
        copy = pltpu.make_async_remote_copy(
            src_ref=src, dst_ref=dst, send_sem=send_sem.at[at], recv_sem=recv_sem.at[at],
            device_id=peer, device_id_type=pl.DeviceIdType.MESH,
        )
        copy.start()
        sent.append(copy)
        return copy

    def copy_in(src, dst):
        copy = pltpu.make_async_copy(src, dst, local_sem.at[len(locals_)])
        copy.start()
        locals_.append(copy)
        return copy

    in_r = [copy_in(r1_in, r_v.at[:, 0:512]), copy_in(r0_in, r_v.at[:, 512:1024])]
    in_a = copy_in(a_in, a_v)
    in_k = [copy_in(k1_in, k_v.at[:, 0:512]), copy_in(k0_in, k_v.at[:, 512:1024])]
    in_p = [copy_in(p1_in, p1_v), copy_in(p0_in, p0_v)]
    in_m = [copy_in(inv1_in, inv1), copy_in(cross_in, cross), copy_in(inv0_in, inv0)]

    barrier = pltpu.get_barrier_semaphore()
    peers = [{"core": other}]
    peers += [{"x": plus("x", s)} for s in (1, 2, 3)]
    peers += [{"y": plus("y", s)} for s in (1, 2, 3)]
    peers += [{"z": plus("z", s)} for s in range(1, 8)]
    for peer in peers:
        pl.semaphore_signal(barrier, inc=1, device_id=peer, device_id_type=pl.DeviceIdType.MESH)

    def half(index):
        return pl.ds(pl.multiple_of(index * 512, 512), 512)

    for copy in (*in_r, in_a):
        copy.wait()
    to_core = []
    for j in range(4):
        c_send[j] = -dot_t(a_v[:, half(other)], r_v[:, 256 * j : 256 * j + 256])
        if j == 0:
            pl.semaphore_wait(barrier, len(peers))
        to_core.append(send(c_send.at[j], c_recv.at[j], core=other))
    for j in range(4):
        c_sum[j] = -dot_t(a_v[:, half(core)], r_v[:, 256 * j : 256 * j + 256])

    def rows_at(index, size, extra=0, count=None):
        start = pl.multiple_of(index * size + extra, 8)
        return pl.ds(start, size if count is None else count)

    def x_stream(j):
        to_core[j].wait_recv()
        c_sum[j] = c_sum[j] + c_recv[j]
        p = send(c_sum.at[j, rows_at(xf, 128, 0, 64)], x1_recv.at[j, 0], x=xp)
        m = send(c_sum.at[j, rows_at(xf, 128, 64, 64)], x1_recv.at[j, 1], x=xm)
        yield
        p.wait_recv()
        at = rows_at(xp, 128, 0, 64)
        c_sum[j, at] = c_sum[j, at] + x1_recv[j, 0]
        p = send(c_sum.at[j, rows_at(xp, 128)], x2_recv.at[j, 0], x=xp)
        m.wait_recv()
        at = rows_at(xm, 128, 64, 64)
        c_sum[j, at] = c_sum[j, at] + x1_recv[j, 1]
        m = send(c_sum.at[j, rows_at(xm, 128)], x2_recv.at[j, 1], x=xm)
        yield
        p.wait_recv()
        m.wait_recv()
        base = core * 512
        own = pl.ds(pl.multiple_of(base + x * 128, 128), 128)
        col[j, own] = c_sum[j, rows_at(x, 128)] + x2_recv[j, 0] + x2_recv[j, 1]
        p = send(col.at[j, own], col.at[j, own], x=xp)
        m = send(col.at[j, own], col.at[j, own], x=xm)
        yield
        p.wait_recv()
        at = pl.ds(pl.multiple_of(base + xm * 128, 64), 64)
        p = send(col.at[j, at], col.at[j, at], x=xp)
        m.wait_recv()
        at = pl.ds(pl.multiple_of(base + xp * 128 + 64, 64), 64)
        m = send(col.at[j, at], col.at[j, at], x=xm)
        yield
        p.wait_recv()
        m.wait_recv()
        c = send(col.at[j, half(core)], col.at[j, half(core)], core=other)
        yield
        c.wait_recv()
        yield

    def z_ring(q, recv, size):
        h = size // 2
        far = plus("z", 4)
        p = send(q.at[far, 0:h], recv.at[0, 0, 0:h], z=plus("z", 1))
        m = send(q.at[far, h:size], recv.at[1, 0, 0:h], z=plus("z", -1))
        yield
        for s in (1, 2, 3):
            to_p, to_m = plus("z", 4 - s), plus("z", s - 4)
            p.wait_recv()
            if s == 1:
                q[to_p, 0:h] = q[to_p, 0:h] + recv[0, 0, 0:h]
            else:
                q[to_p] = q[to_p] + recv[0, s - 1]
            p = send(q.at[to_p], recv.at[0, s], z=plus("z", 1))
            m.wait_recv()
            if s == 1:
                q[to_m, h:size] = q[to_m, h:size] + recv[1, 0, 0:h]
            else:
                q[to_m] = q[to_m] + recv[1, s - 1]
            m = send(q.at[to_m], recv.at[1, s], z=plus("z", -1))
            yield
        p.wait_recv()
        m.wait_recv()

    z_panel, y_panel = (0, 1) if Z_FIRST == 1 else (1, 0)

    def a_stream(i):
        lanes = slice(256 * i, 256 * i + 256)
        first = 512 * z_panel + 256 * i
        t, ty = t_z.at[i], t_zy.at[i]
        t[...] = dot(a_v[...], k_v[:, first : first + 256]).reshape(8, 128, 256)
        yield from z_ring(t, zz_recv.at[i], 128)
        ty[...] = (t[z] + zz_recv[i, 0, 3] + zz_recv[i, 1, 3]).reshape(4, 32, 256)
        p = send(ty.at[yf, 0:16], zy1_recv.at[i, 0], y=yp)
        m = send(ty.at[yf, 16:32], zy1_recv.at[i, 1], y=ym)
        yield
        p.wait_recv()
        ty[yp, 0:16] = ty[yp, 0:16] + zy1_recv[i, 0]
        p = send(ty.at[yp], zy2_recv.at[i, 0], y=yp)
        m.wait_recv()
        ty[ym, 16:32] = ty[ym, 16:32] + zy1_recv[i, 1]
        m = send(ty.at[ym], zy2_recv.at[i, 1], y=ym)
        yield
        p.wait_recv()
        m.wait_recv()
        trail[z_panel, :, lanes] = ty[y] + zy2_recv[i, 0] + zy2_recv[i, 1]
        yield

    def b_stream(i):
        lanes = slice(256 * i, 256 * i + 256)
        first = 512 * y_panel + 256 * i
        t, tz = t_y.at[i], t_yz.at[i]
        t[...] = dot(a_v[...], k_v[:, first : first + 256]).reshape(8, 4, 32, 256)
        p = send(t.at[0:4, yf], yy1_recv.at[i, 0], y=yp)
        m = send(t.at[4:8, yf], yy1_recv.at[i, 1], y=ym)
        yield
        p.wait_recv()
        t[0:4, yp] = t[0:4, yp] + yy1_recv[i, 0]
        p = send(t.at[:, yp], yy2_recv.at[i, 0], y=yp)
        m.wait_recv()
        t[4:8, ym] = t[4:8, ym] + yy1_recv[i, 1]
        m = send(t.at[:, ym], yy2_recv.at[i, 1], y=ym)
        yield
        p.wait_recv()
        m.wait_recv()
        tz[...] = t[:, y] + yy2_recv[i, 0] + yy2_recv[i, 1]
        yield from z_ring(tz, yz_recv.at[i], 32)
        trail[y_panel, :, lanes] = tz[z] + yz_recv[i, 0, 3] + yz_recv[i, 1, 3]
        yield

    def gram():
        at = pl.ds(pl.multiple_of((z * 4 + y) * 32, 32), 32)
        k1, k0 = k_v[half(core), 0:512], k_v[half(core), 512:1024]
        r1, r0 = r_v[at, 0:512], r_v[at, 512:1024]
        p1, p0 = p1_v[...], p0_v[...]
        g_v[0, :, 0:256] = dot_t2(k1, c_sum[0]) + dot_t(p1, r1[:, 0:256])
        g_v[0, 256:512, 256:512] = dot_t2(k1[:, 256:512], c_sum[1]) + dot_t(p1[:, 256:512], r1[:, 256:512])
        for j in (0, 1):
            lanes = slice(256 * j, 256 * j + 256)
            g_v[1, :, lanes] = dot_t2(k1, c_sum[2 + j]) + dot_t(p1, r0[:, lanes])
        g_v[2, :, 0:256] = dot_t2(k0, c_sum[2]) + dot_t(p0, r0[:, 0:256])
        g_v[2, 256:512, 256:512] = dot_t2(k0[:, 256:512], c_sum[3]) + dot_t(p0[:, 256:512], r0[:, 256:512])

    def lower_t(inv, g, whole):
        upper = dot_t3(inv[:, 0:256], g[:, 0:512] if whole else g[:, 0:256])
        lower = dot_t3(inv[256:512, 256:512], g[256:512, 0:512])
        return upper, lower

    def put_tiles(at, upper, lower):
        for index, (i, j) in enumerate(TILES):
            v = upper if i < 2 else lower
            v = v[128 * (i % 2) : 128 * (i % 2) + 128, 128 * j : 128 * j + 128]
            if i == j:
                row = lax.broadcasted_iota(jnp.int32, (128, 128), 0)
                lane = lax.broadcasted_iota(jnp.int32, (128, 128), 1)
                v = jnp.where(row >= lane, v, 0.0)
            d_part[at, 128 * index : 128 * index + 128] = -v

    def local_diag():
        put_tiles(0, *lower_t(inv1[...], g_v[0], False))
        w_upper, w_lower = lower_t(inv1[...], g_v[1], True)
        g_v[1, 0:256] = w_upper
        g_v[1, 256:512] = w_lower
        g_v[2, :, 0:256] = g_v[2, :, 0:256] - dot_t3(cross[...], g_v[1, :, 0:256])
        g_v[2, 256:512, 256:512] = g_v[2, 256:512, 256:512] - dot_t3(cross[:, 256:512], g_v[1, :, 256:512])
        put_tiles(1, *lower_t(inv0[...], g_v[2], False))

    def d_stream(i):
        size, base = (768, 512)[i], (0, 768)[i]
        ny, nz = size // 4, size // 32
        whole, by, bz = pl.ds(base, size), pl.ds(base // 4, ny), pl.ds(base // 32, nz)

        def of_y(index, start):
            return pl.ds(pl.multiple_of(start + index * ny, 8), ny)

        def of_z(index, start):
            return pl.ds(pl.multiple_of(start + index * nz, 8), nz)

        c = send(d_part.at[other, whole], d_core.at[whole], core=other)
        yield
        c.wait_recv()
        d_sum[whole] = d_part[core, whole] + d_core[whole]
        cs = [send(d_sum.at[of_y(plus("y", s), base)], dy_recv.at[s - 1, by], y=plus("y", s)) for s in (1, 2, 3)]
        yield
        for c in cs:
            c.wait_recv()
        d_y[by] = d_sum[of_y(y, base)] + dy_recv[0, by] + dy_recv[1, by] + dy_recv[2, by]
        cs = [send(d_y.at[of_z(plus("z", s), base // 4)], dz_recv.at[s - 1, bz], z=plus("z", s)) for s in range(1, 8)]
        yield
        for c in cs:
            c.wait_recv()
        total = d_y[of_z(z, base // 4)]
        for s in range(7):
            total = total + dz_recv[s, bz]
        d_x[x, bz] = total
        cs = [send(d_x.at[x, bz], d_x.at[x, bz], x=plus("x", s)) for s in (1, 2, 3)]
        yield
        for c in cs:
            c.wait_recv()
        own = pl.ds(pl.multiple_of(base + y * ny + z * nz, 8), nz)
        d_all[core, own] = (d_x[0, bz] + d_x[1, bz]) + (d_x[2, bz] + d_x[3, bz])
        cs = [send(d_all.at[core, own], d_all.at[core, own], z=plus("z", s)) for s in range(1, 8)]
        yield
        for c in cs:
            c.wait_recv()
        own = of_y(y, base)
        cs = [send(d_all.at[core, own], d_all.at[core, own], y=plus("y", s)) for s in (1, 2, 3)]
        yield
        for c in cs:
            c.wait_recv()
        c = send(d_all.at[core, whole], d_all.at[core, whole], core=other)
        yield
        c.wait_recv()
        yield

    def row_adjoints():
        bar1 = p1_v[...].astype(F32) - trail[0]
        row1 = dot_f32(bar1, inv1[...])
        rows[0] = row1
        bar0 = p0_v[...].astype(F32) - trail[1] - dot_f32(row1, cross[...])
        rows[1] = dot_f32(bar0, inv0[...])

    streams = {"x%d" % j: x_stream(j) for j in range(4)}
    for i in range(2):
        streams.update({"a%d" % i: a_stream(i), "b%d" % i: b_stream(i), "d%d" % i: d_stream(i)})
    loaded = len(in_r) + 1
    for name in ORDER:
        if name[0] in "ab" and loaded < len(locals_):
            for copy in locals_[loaded:]:
                copy.wait()
            loaded = len(locals_)
        if name == "g":
            gram()
        elif name == "m":
            local_diag()
        elif name == "r":
            row_adjoints()
        else:
            next(streams[name])
    for copy in sent:
        copy.wait_send()


def place(col, d_all, rows, row1_out, row0_out, col1_out, col0_out, diag1_out, diag0_out, diag, sem):
    copies = []

    def put(src, dst):
        copy = pltpu.make_async_copy(src, dst, sem.at[len(copies)])
        copy.start()
        copies.append(copy)

    for j in range(4):
        out = (col1_out, col0_out)[j // 2]
        put(col.at[j], out.at[:, 256 * (j % 2) : 256 * (j % 2) + 256])
    put(rows.at[0], row1_out)
    put(rows.at[1], row0_out)
    for panel, out in enumerate((diag1_out, diag0_out)):
        for i in range(3):
            diag[panel, 128 * i : 128 * i + 128, 128 * i + 128 : 512] = jnp.zeros((128, 384 - 128 * i), F32)
        for index, (i, j) in enumerate(TILES):
            tile = d_all[panel, 128 * index : 128 * index + 128]
            diag[panel, 128 * i : 128 * i + 128, 128 * j : 128 * j + 128] = tile
        put(diag.at[panel], out)
    for copy in copies:
        copy.wait()


def local(adj_trailing, panel_rows0, panel_rows1, panel_cols0, panel_cols1, inv_diag0, inv_diag1, cross_block, panel_adj0, panel_adj1):
    anywhere = pl.BlockSpec(memory_space=pltpu.HBM)
    vmem = pl.BlockSpec(memory_space=pltpu.VMEM)
    out = lambda *dims: jax.ShapeDtypeStruct(dims, F32)
    f = lambda *dims: pltpu.VMEM(dims, F32)
    b = lambda *dims: pltpu.VMEM(dims, BF16)
    results = pl.pallas_call(
        kernel,
        out_shape=(f(4, 1024, 256), f(2, 1280, 128), f(2, 32, 512)),
        in_specs=[anywhere] * 10,
        out_specs=(vmem,) * 3,
        scratch_shapes=[
            b(1024, 1024), b(1024, 1024), b(1024, 1024), f(512, 512), f(512, 512), f(512, 512), b(32, 512), b(32, 512),
            f(4, 512, 256), f(4, 512, 256), f(4, 512, 256), f(4, 2, 64, 256), f(4, 2, 128, 256),
            f(2, 8, 128, 256), f(2, 2, 4, 128, 256), f(2, 4, 32, 256), f(2, 2, 16, 256), f(2, 2, 32, 256),
            f(2, 8, 4, 32, 256), f(2, 2, 4, 32, 256), f(2, 2, 8, 32, 256), f(2, 8, 32, 256), f(2, 2, 4, 32, 256), f(2, 32, 512),
            f(3, 512, 512), f(2, 1280, 128), f(1280, 128), f(1280, 128), f(320, 128), f(3, 320, 128),
            f(7, 40, 128), f(4, 40, 128),
            pltpu.SemaphoreType.DMA((16,)), pltpu.SemaphoreType.DMA((152,)), pltpu.SemaphoreType.DMA((152,)),
        ],
        compiler_params=pltpu.CompilerParams(collective_id=0, has_side_effects=True, vmem_limit_bytes=VMEM_LIMIT),
        name="panels",
    )(
        adj_trailing, panel_rows0, panel_rows1, panel_cols0, panel_cols1,
        inv_diag0, inv_diag1, cross_block, panel_adj0, panel_adj1,
    )
    return pl.pallas_call(
        place,
        out_shape=(out(32, 512), out(32, 512), out(1024, 512), out(1024, 512), out(512, 512), out(512, 512)),
        in_specs=[vmem] * 3,
        out_specs=(anywhere,) * 6,
        scratch_shapes=[f(2, 512, 512), pltpu.SemaphoreType.DMA((8,))],
        compiler_params=pltpu.CompilerParams(vmem_limit_bytes=4 << 20),
        name="place",
    )(*results)


def solution(mesh):
    finer = Mesh(mesh.devices.reshape(SIZES), AXES)
    every = (*ROW, *COL)
    in_specs = (
        P(ROW, COL), P(ROW, None), P(ROW, None), P(COL, None), P(COL, None),
        P(), P(), P(), P(every, None), P(every, None),
    )
    out_specs = (P(every, None), P(every, None), P(COL, None), P(COL, None), P(), P())
    return jax.shard_map(local, mesh=finer, in_specs=in_specs, out_specs=out_specs, check_vma=False)
```
